32 devices in a mesh: grp: 2 (over y), row: 8 (over z, x), col: 2 (over core).
Axes of the slice: x: 2, y: 2, z: 4, core: 2. Of those that a mesh axis runs over, the one named last changes fastest.
Arguments:
- potential: float32 [128, 32, 128], P(('grp', 'row')), parts along dimension 0, may hold values from -6 to 6
- charges_guess: float32 [128, 32, 128], P(('grp', 'row')), parts along dimension 0, may hold values from -4 to 4
- elast_diag: bfloat16 [128, 128, 128], P(('grp', 'row')), parts along dimension 0, as said below
- elast_off: bfloat16 [128, 14, 128, 128], P(('grp', 'row'), 'col'), parts along dimension 0, may hold values from -0.03125 to 0.03125
- factor_diag: bfloat16 [128, 128, 128], P(('grp', 'row')), parts along dimension 0, as said below
- factor_off: bfloat16 [128, 14, 128, 128], P(('grp', 'row'), 'col'), parts along dimension 0, may hold values from -0.0234375 to 0.0234375
- block_slot: int32 [128, 14], P(('grp', 'row'), 'col'), parts along dimension 0, may hold values from 0 to 55, as said below
- need_list: int32 [16, 2, 7, 8], P(('grp', 'row'), 'col'), parts along dimension 0, may hold values from 0 to 7, as said below
Outputs:
- charges: float32 [128, 32, 128], P(('grp', 'row')), parts along dimension 0
- residual: float32 [128, 32, 128], P(('grp', 'row')), parts along dimension 0
The draws below stay inside these ranges and needn't reach their ends.
There are 2 independent parts, one for each index of `grp`. The reference program is written for one: setup_inputs(seed, part) draws one part's arguments, and reference() takes and returns one part's arrays. A program takes and returns all parts, laid end to end along the dimension named above; each array names one. Nothing has to cross between parts.
Inputs may be any that keep to these rules, and one draw needn't show every extreme that they name: `block_slot`: within one device's 8 x 7 slots all positions differ; position t * 8 + j stands for entry j of need_list[s, c, t] with s = (d + t - 3) mod 8. need_list[s, c, t] holds 8 distinct block rows of row index s, numbered within that index. `elast_diag`: each block is symmetric, with diagonal entries near 1.2 to 2.4 and other entries under 0.6 / sqrt(128) in size. `factor_diag`: diagonal entries near 0.6 to 1.0, other entries under 0.6 / sqrt(128) in size.
All inputs are finite; a program needn't handle non-finite values.
Results may differ from the reference program's by a relative error of at most 0.015.
The reference program's roundings to bfloat16 on the way count: a program that leaves them out, or rounds other values in their place, can miss the bound.
Values may be sent and summed in bfloat16 or wider, within the bound.
A program may use at most 64 MiB of HBM per device.

```python
import jax
import jax.numpy as jnp
from jax import lax

BS = 128
NRHS = 32
BR = 8
KC = 7
REACH = 3
ITERS = 3
K = 14
NB = 64
NEAR = 7
S = 8
N_ROW = 8
N_COL = 2


def draw_block_slot(key, part):
    key = jax.random.fold_in(key, 11)
    positions = NEAR * S
    key_list = jax.random.split(key, N_ROW * N_COL)

    def per_device(subkey):
        return jax.random.permutation(subkey, positions)[:BR * KC].astype(jnp.int32)
    chosen = jax.vmap(per_device)(key_list).reshape(N_ROW, N_COL, BR, KC)
    return chosen.transpose(0, 2, 1, 3).reshape(N_ROW * BR, N_COL * KC).astype(jnp.int32)


def draw_need_list(key, part):
    key = jax.random.fold_in(key, 12)
    key_list = jax.random.split(key, N_ROW * N_COL * NEAR)

    def per_list(subkey):
        return jax.random.permutation(subkey, BR)[:S].astype(jnp.int32)
    return jax.vmap(per_list)(key_list).reshape(N_ROW, N_COL, NEAR, S).astype(jnp.int32)


def draw_elast_diag(key, part):
    key = jax.random.fold_in(key, 21)
    first_key, second_key = jax.random.split(key)
    diagonal_values = jax.random.uniform(first_key, (NB, BS), jnp.float32, 1.2, 2.4)
    jitter = jnp.clip(jax.random.normal(second_key, (NB, BS, BS), jnp.float32), -3.0, 3.0)
    symmetric = (jitter + jnp.swapaxes(jitter, 1, 2)) * (0.1 / BS ** 0.5)
    identity = jnp.eye(BS, dtype=jnp.float32)
    return (symmetric + diagonal_values[:, :, None] * identity[None, :, :]).astype(jnp.bfloat16)


def draw_factor_diag(key, part):
    key = jax.random.fold_in(key, 22)
    first_key, second_key = jax.random.split(key)
    diagonal_values = jax.random.uniform(first_key, (NB, BS), jnp.float32, 0.6, 1.0)
    jitter = jnp.clip(jax.random.normal(second_key, (NB, BS, BS), jnp.float32), -3.0, 3.0)
    identity = jnp.eye(BS, dtype=jnp.float32)
    return (jitter * (0.15 / BS ** 0.5) + diagonal_values[:, :, None] * identity[None, :, :]).astype(jnp.bfloat16)


def shard_levels(key, extent, cuts, least, high):
    gain = 1.0
    for position, blocks in cuts:
        heights = jax.random.uniform(jax.random.fold_in(jax.random.fold_in(key, 6), position), (blocks,), jnp.float32, least / len(cuts), high / len(cuts))
        gain = gain * jnp.repeat(jnp.exp(heights), extent[position] // blocks).reshape((-1,) + (1,) * (len(extent) - 1 - position))
    return gain


def gaussian(key, dims, scale, bound, shards=(), kind=jnp.bfloat16):
    drawn = jax.random.normal(key, dims, jnp.float32) * scale
    if len(shards) > 0:
        drawn = shard_levels(key, dims, shards, -0.22, 0.18) * drawn
    return jnp.clip(drawn, min=-bound, max=bound).astype(kind)


def setup_inputs(seed: int = 0, part: int = 0) -> dict:
    keys = jax.random.split(jax.random.key(seed), 9)
    own_keys = jax.random.split(jax.random.fold_in(keys[8], part), 9)
    potential = gaussian(own_keys[0], (NB, NRHS, BS), 1.0, 6.0, ((0, 8),), jnp.float32)
    charges_guess = gaussian(own_keys[1], (NB, NRHS, BS), 0.5, 4.0, ((0, 8),), jnp.float32)
    elast_diag = draw_elast_diag(jax.random.fold_in(jax.random.fold_in(keys[8], part), 71), part)
    elast_off = gaussian(own_keys[3], (NB, K, BS, BS), (18 * K * BS) ** -0.5, 0.03125, ((0, 8), (1, 2)))
    factor_diag = draw_factor_diag(jax.random.fold_in(jax.random.fold_in(keys[8], part), 71), part)
    factor_off = gaussian(own_keys[5], (NB, K, BS, BS), (36 * K * BS) ** -0.5, 0.0234375, ((0, 8), (1, 2)))
    block_slot = draw_block_slot(jax.random.fold_in(jax.random.fold_in(keys[8], part), 71), part)
    need_list = draw_need_list(jax.random.fold_in(jax.random.fold_in(keys[8], part), 71), part)
    return {"potential": potential, "charges_guess": charges_guess, "elast_diag": elast_diag, "elast_off": elast_off, "factor_diag": factor_diag, "factor_off": factor_off, "block_slot": block_slot, "need_list": need_list}


def rounded(values):
    return lax.optimization_barrier(values.astype(jnp.bfloat16)).astype(jnp.float32)


def column_blocks(block_slot, need_list):
    row_owner = (jnp.arange(NB, dtype=jnp.int32) // BR).astype(jnp.int32)
    col_owner = (jnp.arange(K, dtype=jnp.int32) // KC).astype(jnp.int32)
    offset_slot = (block_slot // S).astype(jnp.int32)
    list_slot = (block_slot % S).astype(jnp.int32)
    source_row = ((row_owner[:, None] + offset_slot - REACH) % N_ROW).astype(jnp.int32)
    picked = need_list[source_row, col_owner[None, :], offset_slot, list_slot]
    return (source_row * BR + picked).astype(jnp.int32)


def forward_blocks(off_blocks, columns, vector_bf):
    ghost_blocks = vector_bf[columns]

    def per_group(operand):
        blocks, ghosts = operand
        return jnp.einsum("bkij,bkrj->bri", blocks.astype(jnp.float32), ghosts.astype(jnp.float32),
                          precision=lax.Precision.HIGHEST)

    result = lax.map(per_group, (off_blocks.reshape(N_ROW, BR, K, BS, BS),
                                 ghost_blocks.reshape(N_ROW, BR, K, NRHS, BS)))
    return result.reshape(NB, NRHS, BS)


def returned_blocks(off_blocks, columns, vector_bf):
    def per_group(operand):
        blocks, local = operand
        return jnp.einsum("bkij,bri->bkrj", blocks.astype(jnp.float32), local.astype(jnp.float32),
                          precision=lax.Precision.HIGHEST)

    contribution = lax.map(per_group, (off_blocks.reshape(N_ROW, BR, K, BS, BS),
                                       vector_bf.reshape(N_ROW, BR, NRHS, BS)))
    contribution = rounded(contribution).reshape(NB * K, NRHS, BS)
    return jnp.zeros((NB, NRHS, BS), jnp.float32).at[columns.reshape(-1)].add(contribution)


def diag_product(diagonal, vector_bf, spec):
    return jnp.einsum(spec, diagonal.astype(jnp.float32), vector_bf.astype(jnp.float32),
                      precision=lax.Precision.HIGHEST)


def apply_elast(vector, elast_diag, elast_off, columns):
    vector_bf = vector.astype(jnp.bfloat16)
    total = diag_product(elast_diag, vector_bf, "bij,brj->bri")
    total = total + forward_blocks(elast_off, columns, vector_bf)
    return total + returned_blocks(elast_off, columns, vector_bf)


def apply_precond(vector, factor_diag, factor_off, columns):
    vector_bf = vector.astype(jnp.bfloat16)
    inner_w = diag_product(factor_diag, vector_bf, "bij,brj->bri") + forward_blocks(factor_off, columns, vector_bf)
    inner_bf = inner_w.astype(jnp.bfloat16)
    return diag_product(factor_diag, inner_bf, "bji,brj->bri") + returned_blocks(factor_off, columns, inner_bf)


def reference(potential, charges_guess, elast_diag, elast_off, factor_diag, factor_off, block_slot, need_list):
    columns = column_blocks(block_slot, need_list)
    charges = charges_guess
    residual = potential - apply_elast(charges_guess, elast_diag, elast_off, columns)
    precond = apply_precond(residual, factor_diag, factor_off, columns)
    rz_value = jnp.sum(residual * precond, axis=(0, 2))
    direction = precond
    for sweep_index in range(ITERS):
        image = apply_elast(direction, elast_diag, elast_off, columns)
        step_size = rz_value / jnp.sum(direction * image, axis=(0, 2))
        charges = charges + step_size[None, :, None] * direction
        residual = residual - step_size[None, :, None] * image
        if sweep_index + 1 < ITERS:
            precond = apply_precond(residual, factor_diag, factor_off, columns)
            fresh = jnp.sum(residual * precond, axis=(0, 2))
            direction = precond + (fresh / rz_value)[None, :, None] * direction
            rz_value = fresh
    return charges, residual
```

```python
import functools

import jax
import jax.numpy as jnp
from jax import lax
from jax.experimental import pallas as pl
from jax.experimental.pallas import tpu as pltpu
from jax.sharding import PartitionSpec as P

ITERS = 3
F32 = jnp.float32
BF16 = jnp.bfloat16


def mm(a, b):
    return lax.dot_general(a, b, (((1,), (0,)), ((), ())), preferred_element_type=F32)


def mm_t(a, b):
    return lax.dot_general(a, b, (((1,), (1,)), ((), ())), preferred_element_type=F32)


def kernel(
    rows_n, near, half,
    take_ref, brow_ref, pot_ref, guess_ref, ediag_ref, eoff_ref, fdiag_ref, foff_ref,
    charges_ref, resid_ref,
    w_ref, stage_ref, ghost_ref, full_ref, rout_ref, rin_ref, pout_ref, pin_ref, ar_ref,
    w_send, w_recv, g_send, g_recv, f_send, f_recv, r_send, r_recv, p_send, p_recv,
    a_send, a_recv, o_send, o_recv,
):
    d = lax.axis_index("row")
    h = lax.axis_index("col")
    sib = 1 - h
    reach = (near - 1) // 2
    group = rows_n * 2
    me = d * 2 + h
    rhs, atoms = pot_ref.shape[1], pot_ref.shape[2]
    per = near * half
    mine = pl.ds(h * half, half)
    theirs = pl.ds(sib * half, half)

    barrier = pltpu.get_barrier_semaphore()

    def greet(o, c):
        other = lax.rem(me + o, group)
        pl.semaphore_signal(
            barrier, inc=1, device_id={"row": other // 2, "col": lax.rem(other, 2)},
            device_id_type=pl.DeviceIdType.MESH)
        return c

    lax.fori_loop(1, group, greet, 0)

    def pick_other(m, off_ref):
        def body(n, c):
            stage_ref[m, n] = off_ref[take_ref[per + n]]
            return c
        lax.fori_loop(0, per, body, 0)

    def pick_own(m, off_ref):
        def body(n, c):
            w_ref[m, 0, n] = off_ref[take_ref[n]]
            return c
        lax.fori_loop(0, per, body, 0)

    def remote(src, dst, ssem, rsem, row, col):
        return pltpu.make_async_remote_copy(
            src_ref=src, dst_ref=dst, send_sem=ssem, recv_sem=rsem,
            device_id={"row": row, "col": col}, device_id_type=pl.DeviceIdType.MESH)

    def weights(m):
        return remote(stage_ref.at[m], w_ref.at[m, 1], w_send.at[m], w_recv.at[m], d, sib)

    pick_other(0, eoff_ref)
    pl.semaphore_wait(barrier, group - 1)
    weights(0).start()

    def order(q):
        return reach + (1 - 2 * lax.rem(q, 2)) * ((q + 1) // 2)

    def ghost_copy(e, t):
        row = lax.rem(d + reach - t + rows_n, rows_n)
        return remote(ghost_ref.at[e, reach], ghost_ref.at[e, t], g_send.at[e, t], g_recv.at[e, t], row, h)

    def full_copy(e):
        return remote(full_ref.at[e, mine], full_ref.at[e, mine], f_send.at[e], f_recv.at[e], d, sib)

    def ret_copy(e, t):
        row = lax.rem(d + t - reach + rows_n, rows_n)
        return remote(rout_ref.at[e, t], rin_ref.at[e, t], r_send.at[e, t], r_recv.at[e, t], row, h)

    def part_copy(e):
        return remote(pout_ref.at[e, theirs], pin_ref.at[e], p_send.at[e], p_recv.at[e], d, sib)

    def loop_q(body):
        def step(q, c):
            body(order(q))
            return c
        lax.fori_loop(1, near, step, 0)

    def fetch_start(e, vb):
        ghost_ref[e, reach] = vb
        loop_q(lambda t: ghost_copy(e, t).start())

    def transposed(e):
        def one(t):
            for r in range(half):
                n = t * half + r
                first = mm(full_ref[e, brow_ref[n]], w_ref[e, 0, n]).astype(BF16).astype(F32)
                second = mm(full_ref[e, brow_ref[per + n]], w_ref[e, 1, n]).astype(BF16).astype(F32)
                rout_ref[e, t, r] = (first + second).astype(BF16)

        def far(t):
            one(t)
            ret_copy(e, t).start()
        loop_q(far)
        one(reach)

    def forward(e):
        blocks = 2 * half

        def one(t, acc):
            acc = list(acc)
            for r in range(half):
                n = t * half + r
                both = jnp.concatenate([w_ref[e, 0, n], w_ref[e, 1, n]], axis=0)
                got = mm_t(ghost_ref[e, t, r], both)
                for side in range(2):
                    piece = got[:, side * atoms:(side + 1) * atoms]
                    b = brow_ref[side * per + n]
                    for row in range(blocks):
                        acc[row] = acc[row] + jnp.where(b == row, piece, 0.0)
            return tuple(acc)

        acc = one(reach, tuple(jnp.zeros((rhs, atoms), F32) for _ in range(blocks)))

        def step(q, acc):
            t = order(q)
            ghost_copy(e, t).wait_recv()
            return one(t, acc)

        acc = lax.fori_loop(1, near, step, acc)
        for row in range(blocks):
            pout_ref[e, row] = acc[row]
        part_copy(e).start()

    def diag(ref, vb, transpose):
        out = []
        for r in range(half):
            block = ref[h * half + r]
            out.append(mm(vb[r], block) if transpose else mm_t(vb[r], block))
        return jnp.stack(out)

    def returned(e):
        total = rout_ref[e, reach].astype(F32)
        for q in range(1, near):
            t = reach + (1 - 2 * (q % 2)) * ((q + 1) // 2)
            ret_copy(e, t).wait_recv()
            total = total + rin_ref[e, t].astype(F32)
        return total

    def drain(e):
        def one(t):
            ghost_copy(e, t).wait_send()
            ret_copy(e, t).wait_send()
        loop_q(one)
        full_copy(e).wait_send()
        part_copy(e).wait_send()

    def elast(v):
        e = 0
        vb = v.astype(BF16)
        full_ref[e, mine] = vb
        full_copy(e).start()
        fetch_start(e, vb)
        return vb

    def elast_end(vb):
        e = 0
        full_copy(e).wait_recv()
        transposed(e)
        dpart = diag(ediag_ref, vb, False)
        forward(e)
        total = dpart + returned(e)
        part_copy(e).wait_recv()
        total = total + (pout_ref[e, mine] + pin_ref[e])
        drain(e)
        return total

    def factor(v, after_start=None):
        e = 1
        vb = v.astype(BF16)
        fetch_start(e, vb)
        if after_start is not None:
            after_start()
        dpart = diag(fdiag_ref, vb, False)
        forward(e)
        part_copy(e).wait_recv()
        w = dpart + (pout_ref[e, mine] + pin_ref[e])
        wb = w.astype(BF16)
        full_ref[e, mine] = wb
        full_copy(e).start()
        dpart = diag(fdiag_ref, wb, True)
        full_copy(e).wait_recv()
        transposed(e)
        total = dpart + returned(e)
        drain(e)
        return total

    count = [0]

    def dot(a, b):
        par = count[0] % 2
        count[0] += 1
        s = jnp.sum(a * b, axis=0)
        s = jnp.concatenate([s, jnp.zeros((atoms - rhs, atoms), F32)], axis=0)
        ar_ref[par, 0] = jnp.sum(s.T, axis=0, keepdims=True)

        def copy(o):
            other = lax.rem(me + o, group)
            return remote(ar_ref.at[par, 0], ar_ref.at[par, o], a_send.at[par, o], a_recv.at[par, o],
                          other // 2, lax.rem(other, 2))

        def start(o, c):
            copy(o).start()
            return c

        def finish(o, c):
            copy(o).wait()
            return c

        lax.fori_loop(1, group, start, 0)
        lax.fori_loop(1, group, finish, 0)
        total = jnp.sum(ar_ref[par], axis=0)
        return jnp.broadcast_to(total, (atoms, atoms)).T[:rhs]

    guess = guess_ref[mine]
    vb = elast(guess)
    pick_own(0, eoff_ref)
    pick_other(1, foff_ref)
    weights(1).start()
    pick_own(1, foff_ref)
    weights(0).wait()
    residual = pot_ref[mine] - elast_end(vb)
    precond = factor(residual, lambda: weights(1).wait())
    rz = dot(residual, precond)
    resid_ref[mine] = residual
    charges_ref[mine] = guess
    direction = precond
    for sweep in range(ITERS):
        image = elast_end(elast(direction))
        step = rz / dot(direction, image)
        charges_ref[mine] = charges_ref[mine] + step[None] * direction
        residual = resid_ref[mine] - step[None] * image
        resid_ref[mine] = residual
        if sweep + 1 < ITERS:
            precond = factor(residual)
            fresh = dot(residual, precond)
            direction = precond + (fresh / rz)[None] * direction
            rz = fresh
    last = [
        remote(ref.at[mine], ref.at[mine], o_send.at[i], o_recv.at[i], d, sib)
        for i, ref in enumerate((charges_ref, resid_ref))
    ]
    for copy in last:
        copy.start()
    for copy in last:
        copy.wait()


def local(
    potential, charges_guess, elast_diag, elast_off, factor_diag, factor_off, block_slot, need_list
):
    rows_n = lax.axis_size("row")
    near, width = need_list.shape[2], need_list.shape[3]
    reach = (near - 1) // 2
    block_rows, slot_count = block_slot.shape
    rhs, atoms = potential.shape[1], potential.shape[2]
    slots = block_rows * slot_count
    assert slots == near * width and width == block_rows and lax.axis_size("col") == 2
    half = block_rows // 2
    per = near * half
    d = lax.axis_index("row")
    h = lax.axis_index("col")

    flat = block_slot.reshape(-1)
    i32 = jnp.int32
    slot_at = jnp.sum(
        jnp.where(flat[None, :] == jnp.arange(slots, dtype=i32)[:, None], jnp.arange(slots, dtype=i32)[None, :], 0),
        axis=1)
    needs = need_list[0, 0]
    at = jnp.arange(width, dtype=i32)
    place = jnp.sum(jnp.where(needs[:, None, :] == at[None, :, None], at[None, None, :], 0), axis=2)
    both = jnp.concatenate([slot_at, place.reshape(-1)])
    every = lax.all_gather(both, ("row", "col")).reshape(rows_n, 2, 2 * slots)
    wrapped = jnp.concatenate([every[-reach:], every, every[:reach]], axis=0) if rows_n > 1 else every
    window = lax.dynamic_slice_in_dim(wrapped, d, near, axis=0)
    slot_both = lax.dynamic_index_in_dim(every, d, axis=0, keepdims=False)[:, :slots]
    ids = jnp.arange(near)
    place_both = window[:, :, slots:].reshape(near, 2, near, width)[ids, :, ids].transpose(1, 0, 2)
    pos = place_both + (jnp.arange(near, dtype=i32) * width)[None, :, None]
    pos = pos.reshape(2, slots)
    hit = pos[:, :, None] == jnp.arange(slots, dtype=i32)[None, None, :]
    item = jnp.sum(jnp.where(hit, slot_both[:, None, :], 0), axis=2).reshape(2, near, 2, half)
    own = jnp.where(h == 0, item[0], item[1])
    other = jnp.where(h == 0, item[1], item[0])

    def in_half(x, which):
        return jnp.where(which == 0, x[:, 0], x[:, 1]).reshape(-1)

    take = jnp.concatenate([in_half(own, h), in_half(own, 1 - h)])
    brow = jnp.concatenate([in_half(own, h), in_half(other, h)]) // slot_count

    vmem = pl.BlockSpec(memory_space=pltpu.VMEM)
    smem = pl.BlockSpec(memory_space=pltpu.SMEM)
    group = rows_n * 2
    dma = pltpu.SemaphoreType.DMA
    shape = jax.ShapeDtypeStruct(potential.shape, F32)
    return pl.pallas_call(
        functools.partial(kernel, rows_n, near, half),
        out_shape=(shape, shape),
        in_specs=[smem, smem] + [vmem] * 6,
        out_specs=(vmem, vmem),
        scratch_shapes=[
            pltpu.VMEM((2, 2, per, atoms, atoms), BF16),
            pltpu.VMEM((2, per, atoms, atoms), BF16),
            pltpu.VMEM((2, near, half, rhs, atoms), BF16),
            pltpu.VMEM((2, block_rows, rhs, atoms), BF16),
            pltpu.VMEM((2, near, half, rhs, atoms), BF16),
            pltpu.VMEM((2, near, half, rhs, atoms), BF16),
            pltpu.VMEM((2, block_rows, rhs, atoms), F32),
            pltpu.VMEM((2, half, rhs, atoms), F32),
            pltpu.VMEM((2, group, 1, atoms), F32),
            dma((2,)), dma((2,)),
            dma((2, near)), dma((2, near)),
            dma((2,)), dma((2,)),
            dma((2, near)), dma((2, near)),
            dma((2,)), dma((2,)),
            dma((2, group)), dma((2, group)),
            dma((2,)), dma((2,)),
        ],
        compiler_params=pltpu.CompilerParams(
            collective_id=0, has_side_effects=True, vmem_limit_bytes=48 * 1024 * 1024),
    )(
        take, brow, potential, charges_guess, elast_diag,
        elast_off.reshape(slots, atoms, atoms), factor_diag, factor_off.reshape(slots, atoms, atoms),
    )


def solution(mesh):
    return jax.shard_map(
        local,
        mesh=mesh,
        in_specs=(
            P(("grp", "row"), None, None),
            P(("grp", "row"), None, None),
            P(("grp", "row"), None, None),
            P(("grp", "row"), "col", None, None),
            P(("grp", "row"), None, None),
            P(("grp", "row"), "col", None, None),
            P(("grp", "row"), "col"),
            P(("grp", "row"), "col", None, None),
        ),
        out_specs=(P(("grp", "row"), None, None), P(("grp", "row"), None, None)),
        check_vma=False,
    )
```

```python
import functools

import jax
import jax.numpy as jnp
from jax import lax
from jax.experimental import pallas as pl
from jax.experimental.pallas import tpu as pltpu
from jax.sharding import PartitionSpec as P

ITERS = 3
F32 = jnp.float32
BF16 = jnp.bfloat16


def mm(a, b):
    return lax.dot_general(a, b, (((1,), (0,)), ((), ())), preferred_element_type=F32)


def mm_t(a, b):
    return lax.dot_general(a, b, (((1,), (1,)), ((), ())), preferred_element_type=F32)


def kernel(
    rows_n, near, half,
    slot_ref, need_ref, pot_hbm, guess_hbm, ediag_hbm, eoff_hbm, fdiag_hbm, foff_hbm,
    charges_ref, resid_ref,
    take_ref, brow_ref, msg_ref, list_ref, table_ref,
    pot_ref, guess_ref, ediag_ref, eoff_ref, fdiag_ref, foff_ref,
    in_sem, m_send, m_recv, t_sem,
    w_ref, stage_ref, ghost_ref, full_e_ref, full_f_ref, rout_ref, rin_ref, pout_ref, pin_ref, ar_ref,
    w_send, w_recv, g_send, g_recv, f_send, f_recv, r_send, r_recv, p_send, p_recv,
    a_send, a_recv, o_send, o_recv,
):
    full_refs = (full_e_ref, full_f_ref)
    d = lax.axis_index("row")
    h = lax.axis_index("col")
    sib = 1 - h
    reach = (near - 1) // 2
    group = rows_n * 2
    me = d * 2 + h
    rhs, atoms = pot_ref.shape[1], pot_ref.shape[2]
    per = near * half
    mine = pl.ds(h * half, half)
    theirs = pl.ds(sib * half, half)

    loads = [
        pltpu.make_async_copy(src, dst, in_sem.at[i])
        for i, (src, dst) in enumerate((
            (guess_hbm, guess_ref), (eoff_hbm, eoff_ref), (foff_hbm, foff_ref),
            (pot_hbm, pot_ref), (ediag_hbm, ediag_ref), (fdiag_hbm, fdiag_ref)))
    ]
    for load in loads:
        load.start()

    barrier = pltpu.get_barrier_semaphore()

    def greet(o, c):
        other = lax.rem(me + o, group)
        pl.semaphore_signal(
            barrier, inc=1, device_id={"row": other // 2, "col": lax.rem(other, 2)},
            device_id_type=pl.DeviceIdType.MESH)
        return c

    lax.fori_loop(1, group, greet, 0)

    def pick_other(m, off_ref):
        def body(n, c):
            stage_ref[m, n] = off_ref[take_ref[per + n]]
            return c
        lax.fori_loop(0, per, body, 0)

    def pick_own(m, off_ref):
        def body(n, c):
            w_ref[m, 0, n] = off_ref[take_ref[n]]
            return c
        lax.fori_loop(0, per, body, 0)

    def remote(src, dst, ssem, rsem, row, col):
        return pltpu.make_async_remote_copy(
            src_ref=src, dst_ref=dst, send_sem=ssem, recv_sem=rsem,
            device_id={"row": row, "col": col}, device_id_type=pl.DeviceIdType.MESH)

    def weights(m):
        return remote(stage_ref.at[m], w_ref.at[m, 1], w_send.at[m], w_recv.at[m], d, sib)

    block_rows, slot_count = slot_ref.shape
    width = need_ref.shape[1]
    lane = lax.broadcasted_iota(jnp.int32, (block_rows, atoms), 1)
    line = lax.broadcasted_iota(jnp.int32, (block_rows, atoms), 0)
    slot_at = jnp.zeros((block_rows, atoms), jnp.int32)
    for k in range(slot_count):
        slot_at = slot_at + jnp.where(slot_ref[:, k:k + 1] == lane, line * slot_count + k, 0)
    slot_at = jnp.sum(slot_at, axis=0, keepdims=True)
    lane = lax.broadcasted_iota(jnp.int32, (near, atoms), 1)
    place = jnp.zeros((near, atoms), jnp.int32)
    for j in range(width):
        place = place + jnp.where(need_ref[:, j:j + 1] == lane, j, 0)
    msg_ref[0, reach] = jnp.concatenate([place, slot_at], axis=0)

    def msg_copy(k, t):
        row = lax.rem(d + reach - t + rows_n, rows_n)
        return remote(msg_ref.at[0, reach], msg_ref.at[k, t], m_send.at[k, t], m_recv.at[k, t],
                      row, lax.rem(h + k, 2))

    messages = [(k, t) for k in range(2) for t in range(near) if (k, t) != (0, reach)]

    def read_lists():
        for k, t in messages:
            msg_copy(k, t).wait()
        list_ref[...] = jnp.concatenate(
            [line for k in range(2)
             for line in [msg_ref[k, t, t:t + 1] for t in range(near)] + [msg_ref[k, reach, near:near + 1]]],
            axis=0)
        copy = pltpu.make_async_copy(list_ref, table_ref, t_sem.at[0])
        copy.start()
        copy.wait()

        def fill(n, c):
            t = n // half
            r = lax.rem(n, half)

            def slot_of(k, side):
                at = jnp.clip(table_ref[k * (near + 1) + t, side * half + r], 0, width - 1)
                return jnp.clip(table_ref[k * (near + 1) + near, t * width + at], 0, 2 * per - 1)

            own = slot_of(0, h)
            take_ref[n] = own
            take_ref[per + n] = slot_of(0, sib)
            brow_ref[n] = own // slot_count
            brow_ref[per + n] = slot_of(1, h) // slot_count
            return c

        lax.fori_loop(0, per, fill, 0)

    pl.semaphore_wait(barrier, group - 1)
    for k, t in messages:
        msg_copy(k, t).start()

    def order(q):
        return reach + (1 - 2 * lax.rem(q, 2)) * ((q + 1) // 2)

    def ghost_copy(e, t):
        row = lax.rem(d + reach - t + rows_n, rows_n)
        return remote(ghost_ref.at[e, reach], ghost_ref.at[e, t], g_send.at[e, t], g_recv.at[e, t], row, h)

    def full_copy(e):
        return remote(full_refs[e].at[mine], full_refs[e].at[mine], f_send.at[e], f_recv.at[e], d, sib)

    def ret_copy(e, t):
        row = lax.rem(d + t - reach + rows_n, rows_n)
        return remote(rout_ref.at[e, t], rin_ref.at[e, t], r_send.at[e, t], r_recv.at[e, t], row, h)

    def part_copy(e):
        return remote(pout_ref.at[e, theirs], pin_ref.at[e], p_send.at[e], p_recv.at[e], d, sib)

    def loop_q(body):
        def step(q, c):
            body(order(q))
            return c
        lax.fori_loop(1, near, step, 0)

    def fetch_start(e, vb):
        ghost_ref[e, reach] = vb
        loop_q(lambda t: ghost_copy(e, t).start())

    def transposed(e):
        def one(t):
            for r in range(half):
                n = t * half + r
                first = mm(full_refs[e][brow_ref[n]], w_ref[e, 0, n]).astype(BF16).astype(F32)
                second = mm(full_refs[e][brow_ref[per + n]], w_ref[e, 1, n]).astype(BF16).astype(F32)
                rout_ref[e, t, r] = (first + second).astype(BF16)

        def far(t):
            one(t)
            ret_copy(e, t).start()
        loop_q(far)
        one(reach)

    def forward(e):
        blocks = 2 * half

        def one(t, acc):
            acc = list(acc)
            for r in range(half):
                n = t * half + r
                both = jnp.concatenate([w_ref[e, 0, n], w_ref[e, 1, n]], axis=0)
                got = mm_t(ghost_ref[e, t, r], both)
                for side in range(2):
                    piece = got[:, side * atoms:(side + 1) * atoms]
                    b = brow_ref[side * per + n]
                    for row in range(blocks):
                        acc[row] = acc[row] + jnp.where(b == row, piece, 0.0)
            return tuple(acc)

        acc = one(reach, tuple(jnp.zeros((rhs, atoms), F32) for _ in range(blocks)))

        def step(q, acc):
            t = order(q)
            ghost_copy(e, t).wait_recv()
            return one(t, acc)

        acc = lax.fori_loop(1, near, step, acc)
        for row in range(blocks):
            pout_ref[e, row] = acc[row]
        part_copy(e).start()

    def diag(ref, vb, transpose):
        out = []
        for r in range(half):
            block = ref[h * half + r]
            out.append(mm(vb[r], block) if transpose else mm_t(vb[r], block))
        return jnp.stack(out)

    def returned(e):
        total = rout_ref[e, reach].astype(F32)
        for q in range(1, near):
            t = reach + (1 - 2 * (q % 2)) * ((q + 1) // 2)
            ret_copy(e, t).wait_recv()
            total = total + rin_ref[e, t].astype(F32)
        return total

    def drain(e):
        def one(t):
            ghost_copy(e, t).wait_send()
            ret_copy(e, t).wait_send()
        loop_q(one)
        full_copy(e).wait_send()
        part_copy(e).wait_send()

    def elast(v):
        e = 0
        vb = v.astype(BF16)
        full_refs[e][mine] = vb
        full_copy(e).start()
        fetch_start(e, vb)
        return vb

    def elast_end(vb, v=None):
        e = 0
        full_copy(e).wait_recv()
        transposed(e)
        dpart = diag(ediag_ref, vb, False)
        forward(e)
        part_copy(e).wait_recv()
        stored = pout_ref[e, mine] + pin_ref[e]
        finish = None
        if v is not None:
            finish = dot_start(jnp.sum(v * (dpart + 2.0 * stored), axis=0))
        total = dpart + stored + returned(e)
        drain(e)
        return total if finish is None else (total, finish())

    def factor(v, after_start=None):
        e = 1
        vb = v.astype(BF16)
        fetch_start(e, vb)
        if after_start is not None:
            after_start()
        dpart = diag(fdiag_ref, vb, False)
        forward(e)
        part_copy(e).wait_recv()
        w = dpart + (pout_ref[e, mine] + pin_ref[e])
        wb = w.astype(BF16)
        full_refs[e][mine] = wb
        full_copy(e).start()
        finish = dot_start(jnp.sum(w * wb.astype(F32), axis=0))
        dpart = diag(fdiag_ref, wb, True)
        full_copy(e).wait_recv()
        transposed(e)
        total = dpart + returned(e)
        drain(e)
        return total, finish()

    count = [0]

    def dot_start(s):
        par = count[0] % 2
        count[0] += 1
        s = jnp.concatenate([s, jnp.zeros((atoms - rhs, atoms), F32)], axis=0)
        ar_ref[par, 0] = jnp.sum(s.T, axis=0, keepdims=True)

        def copy(o):
            other = lax.rem(me + o, group)
            return remote(ar_ref.at[par, 0], ar_ref.at[par, o], a_send.at[par, o], a_recv.at[par, o],
                          other // 2, lax.rem(other, 2))

        def start(o, c):
            copy(o).start()
            return c

        def finish(o, c):
            copy(o).wait()
            return c

        lax.fori_loop(1, group, start, 0)
        def end():
            lax.fori_loop(1, group, finish, 0)
            total = jnp.sum(ar_ref[par], axis=0)
            return jnp.broadcast_to(total, (atoms, atoms)).T[:rhs]

        return end

    loads[0].wait()
    guess = guess_ref[mine]
    vb = elast(guess)
    read_lists()
    loads[1].wait()
    pick_other(0, eoff_ref)
    weights(0).start()
    loads[2].wait()
    pick_own(0, eoff_ref)
    pick_other(1, foff_ref)
    weights(1).start()
    pick_own(1, foff_ref)
    for load in loads[3:]:
        load.wait()
    weights(0).wait()
    residual = pot_ref[mine] - elast_end(vb)
    precond, rz = factor(residual, lambda: weights(1).wait())
    resid_ref[mine] = residual
    charges_ref[mine] = guess
    direction = precond
    for sweep in range(ITERS):
        image, curvature = elast_end(elast(direction), direction)
        step = rz / curvature
        charges_ref[mine] = charges_ref[mine] + step[None] * direction
        residual = resid_ref[mine] - step[None] * image
        resid_ref[mine] = residual
        if sweep + 1 < ITERS:
            precond, fresh = factor(residual)
            direction = precond + (fresh / rz)[None] * direction
            rz = fresh
    last = [
        remote(ref.at[mine], ref.at[mine], o_send.at[i], o_recv.at[i], d, sib)
        for i, ref in enumerate((charges_ref, resid_ref))
    ]
    for copy in last:
        copy.start()
    for copy in last:
        copy.wait()


def local(
    potential, charges_guess, elast_diag, elast_off, factor_diag, factor_off, block_slot, need_list
):
    rows_n = lax.axis_size("row")
    near, width = need_list.shape[2], need_list.shape[3]
    reach = (near - 1) // 2
    block_rows, slot_count = block_slot.shape
    rhs, atoms = potential.shape[1], potential.shape[2]
    slots = block_rows * slot_count
    assert slots == near * width and width == block_rows and lax.axis_size("col") == 2
    half = block_rows // 2
    per = near * half
    vmem = pl.BlockSpec(memory_space=pltpu.VMEM)
    hbm = pl.BlockSpec(memory_space=pltpu.HBM)
    group = rows_n * 2
    dma = pltpu.SemaphoreType.DMA
    shape = jax.ShapeDtypeStruct(potential.shape, F32)
    return pl.pallas_call(
        functools.partial(kernel, rows_n, near, half),
        out_shape=(shape, shape),
        in_specs=[vmem] * 2 + [hbm] * 6,
        out_specs=(vmem, vmem),
        scratch_shapes=[
            pltpu.SMEM((slots,), jnp.int32), pltpu.SMEM((slots,), jnp.int32),
            pltpu.VMEM((2, near, near + 1, atoms), jnp.int32),
            pltpu.VMEM((2 * (near + 1), atoms), jnp.int32),
            pltpu.SMEM((2 * (near + 1), atoms), jnp.int32),
            pltpu.VMEM(potential.shape, F32), pltpu.VMEM(potential.shape, F32),
            pltpu.VMEM(elast_diag.shape, BF16), pltpu.VMEM((slots, atoms, atoms), BF16),
            pltpu.VMEM(elast_diag.shape, BF16), pltpu.VMEM((slots, atoms, atoms), BF16),
            dma((6,)), dma((2, near)), dma((2, near)), dma((1,)),
            pltpu.VMEM((2, 2, per, atoms, atoms), BF16),
            pltpu.VMEM((2, per, atoms, atoms), BF16),
            pltpu.VMEM((2, near, half, rhs, atoms), BF16),
            pltpu.VMEM((block_rows, rhs, atoms), BF16),
            pltpu.VMEM((block_rows, rhs, atoms), BF16),
            pltpu.VMEM((2, near, half, rhs, atoms), BF16),
            pltpu.VMEM((2, near, half, rhs, atoms), BF16),
            pltpu.VMEM((2, block_rows, rhs, atoms), F32),
            pltpu.VMEM((2, half, rhs, atoms), F32),
            pltpu.VMEM((2, group, 1, atoms), F32),
            dma((2,)), dma((2,)),
            dma((2, near)), dma((2, near)),
            dma((2,)), dma((2,)),
            dma((2, near)), dma((2, near)),
            dma((2,)), dma((2,)),
            dma((2, group)), dma((2, group)),
            dma((2,)), dma((2,)),
        ],
        compiler_params=pltpu.CompilerParams(
            collective_id=0, has_side_effects=True, vmem_limit_bytes=48 * 1024 * 1024),
    )(
        block_slot, need_list.reshape(near, width), potential, charges_guess, elast_diag,
        elast_off.reshape(slots, atoms, atoms), factor_diag, factor_off.reshape(slots, atoms, atoms),
    )


def solution(mesh):
    return jax.shard_map(
        local,
        mesh=mesh,
        in_specs=(
            P(("grp", "row"), None, None),
            P(("grp", "row"), None, None),
            P(("grp", "row"), None, None),
            P(("grp", "row"), "col", None, None),
            P(("grp", "row"), None, None),
            P(("grp", "row"), "col", None, None),
            P(("grp", "row"), "col"),
            P(("grp", "row"), "col", None, None),
        ),
        out_specs=(P(("grp", "row"), None, None), P(("grp", "row"), None, None)),
        check_vma=False,
    )
```

```python
import functools

import jax
import jax.numpy as jnp
from jax import lax
from jax.experimental import pallas as pl
from jax.experimental.pallas import tpu as pltpu
from jax.sharding import PartitionSpec as P

ITERS = 3
F32 = jnp.float32
BF16 = jnp.bfloat16


def mm(a, b):
    return lax.dot_general(a, b, (((1,), (0,)), ((), ())), preferred_element_type=F32)


def mm_t(a, b):
    return lax.dot_general(a, b, (((1,), (1,)), ((), ())), preferred_element_type=F32)


def kernel(
    rows_n, near, half,
    slot_ref, need_ref, pot_hbm, guess_hbm, ediag_hbm, eoff_hbm, fdiag_hbm, foff_hbm,
    charges_ref, resid_ref,
    take_ref, brow_ref, msg_ref, list_ref, table_ref,
    pot_ref, guess_ref, ediag_ref, eoff_ref, fdiag_ref, foff_ref,
    in_sem, m_send, m_recv, t_sem,
    w_ref, stage_ref, ghost_ref, full_e_ref, full_f_ref, rout_ref, rin_ref, pout_ref, pin_ref, ar_ref,
    w_send, w_recv, g_send, g_recv, f_send, f_recv, r_send, r_recv, p_send, p_recv,
    a_send, a_recv, o_send, o_recv,
):
    full_refs = (full_e_ref, full_f_ref)
    d = lax.axis_index("row")
    h = lax.axis_index("col")
    sib = 1 - h
    reach = (near - 1) // 2
    group = rows_n * 2
    rhs, atoms = pot_ref.shape[1], pot_ref.shape[2]
    per = near * half
    mine = pl.ds(h * half, half)
    theirs = pl.ds(sib * half, half)

    loads = [
        pltpu.make_async_copy(src, dst, in_sem.at[i])
        for i, (src, dst) in enumerate((
            (guess_hbm, guess_ref), (eoff_hbm, eoff_ref), (foff_hbm, foff_ref),
            (pot_hbm, pot_ref), (ediag_hbm, ediag_ref), (fdiag_hbm, fdiag_ref)))
    ]
    for load in loads:
        load.start()

    barrier = pltpu.get_barrier_semaphore()

    def wrap(x):
        return jnp.where(x < 0, x + rows_n, jnp.where(x >= rows_n, x - rows_n, x))

    cols = (h, sib)

    def each_other(body):
        body(0, 1, d, sib)
        if rows_n <= 8:
            for o in range(1, rows_n):
                for k in range(2):
                    body(o, k, wrap(d + o), cols[k])
        else:
            def step(o, c):
                for k in range(2):
                    body(o, k, wrap(d + o), cols[k])
                return c
            lax.fori_loop(1, rows_n, step, 0)

    def greet(o, k, row, col):
        pl.semaphore_signal(
            barrier, inc=1, device_id={"row": row, "col": col},
            device_id_type=pl.DeviceIdType.MESH)

    each_other(greet)

    def pick_other(m, off_ref):
        def body(n, c):
            stage_ref[m, n] = off_ref[take_ref[per + n]]
            return c
        lax.fori_loop(0, per, body, 0)

    def pick_own(m, off_ref):
        def body(n, c):
            w_ref[m, 0, n] = off_ref[take_ref[n]]
            return c
        lax.fori_loop(0, per, body, 0)

    def remote(src, dst, ssem, rsem, row, col):
        return pltpu.make_async_remote_copy(
            src_ref=src, dst_ref=dst, send_sem=ssem, recv_sem=rsem,
            device_id={"row": row, "col": col}, device_id_type=pl.DeviceIdType.MESH)

    def weights(m):
        return remote(stage_ref.at[m], w_ref.at[m, 1], w_send.at[m], w_recv.at[m], d, sib)

    block_rows, slot_count = slot_ref.shape
    width = need_ref.shape[1]
    lane = lax.broadcasted_iota(jnp.int32, (block_rows, atoms), 1)
    line = lax.broadcasted_iota(jnp.int32, (block_rows, atoms), 0)
    pad = 1 << (slot_count - 1).bit_length()
    slot_at = jnp.zeros((block_rows, atoms), jnp.int32)
    for k in range(slot_count):
        slot_at = slot_at + jnp.where(slot_ref[:, k:k + 1] == lane, line * pad + k, 0)
    slot_at = jnp.sum(slot_at, axis=0, keepdims=True)
    lane = lax.broadcasted_iota(jnp.int32, (near, atoms), 1)
    place = jnp.zeros((near, atoms), jnp.int32)
    for j in range(width):
        place = place + jnp.where(need_ref[:, j:j + 1] == lane, j, 0)
    msg_ref[0, reach] = jnp.concatenate([place, slot_at], axis=0)

    def msg_copy(k, t):
        row = wrap(d + reach - t)
        return remote(msg_ref.at[0, reach], msg_ref.at[k, t], m_send.at[k, t], m_recv.at[k, t],
                      row, cols[k])

    messages = [(k, t) for k in range(2) for t in range(near) if (k, t) != (0, reach)]

    def read_lists():
        for k, t in messages:
            msg_copy(k, t).wait()
        list_ref[...] = jnp.concatenate(
            [line for k in range(2)
             for line in [msg_ref[k, t, t:t + 1] for t in range(near)] + [msg_ref[k, reach, near:near + 1]]],
            axis=0)
        copy = pltpu.make_async_copy(list_ref, table_ref, t_sem.at[0])
        copy.start()
        copy.wait()

        def slot_of(k, t, side, r):
            at = jnp.clip(table_ref[k * (near + 1) + t, side * half + r], 0, width - 1)
            code = table_ref[k * (near + 1) + near, t * width + at]
            row = jnp.clip(lax.shift_right_arithmetic(code, shift), 0, block_rows - 1)
            return jnp.clip(code - row * (pad - slot_count), 0, 2 * per - 1), row

        shift = pad.bit_length() - 1
        for t in range(near):
            for r in range(half):
                n = t * half + r
                take_ref[n], brow_ref[n] = slot_of(0, t, h, r)
                take_ref[per + n] = slot_of(0, t, sib, r)[0]
                brow_ref[per + n] = slot_of(1, t, h, r)[1]

    pl.semaphore_wait(barrier, group - 1)
    for k, t in messages:
        msg_copy(k, t).start()

    def ghost_copy(e, t):
        row = wrap(d + reach - t)
        return remote(ghost_ref.at[e, reach], ghost_ref.at[e, t], g_send.at[e, t], g_recv.at[e, t], row, h)

    def full_copy(e):
        return remote(full_refs[e].at[mine], full_refs[e].at[mine], f_send.at[e], f_recv.at[e], d, sib)

    def ret_copy(e, t):
        row = wrap(d + t - reach)
        return remote(rout_ref.at[e, t], rin_ref.at[e, t], r_send.at[e, t], r_recv.at[e, t], row, h)

    def part_copy(e):
        return remote(pout_ref.at[e, theirs], pin_ref.at[e], p_send.at[e], p_recv.at[e], d, sib)

    def loop_q(body):
        def step(i, c):
            body(reach - i)
            body(reach + i)
            return c
        lax.fori_loop(1, reach + 1, step, 0)

    def fetch_start(e, vb):
        ghost_ref[e, reach] = vb
        for i in range(1, reach + 1):
            ghost_copy(e, reach - i).start()
            ghost_copy(e, reach + i).start()

    def transposed(e):
        def one(t):
            for r in range(half):
                n = t * half + r
                first = mm(full_refs[e][brow_ref[n]], w_ref[e, 0, n]).astype(BF16).astype(F32)
                second = mm(full_refs[e][brow_ref[per + n]], w_ref[e, 1, n]).astype(BF16).astype(F32)
                rout_ref[e, t, r] = (first + second).astype(BF16)

        def far(t):
            one(t)
            ret_copy(e, t).start()
        loop_q(far)
        one(reach)

    def forward(e):
        blocks = 2 * half

        def one(t, acc):
            acc = list(acc)
            for r in range(half):
                n = t * half + r
                both = jnp.concatenate([w_ref[e, 0, n], w_ref[e, 1, n]], axis=0)
                got = mm_t(ghost_ref[e, t, r], both)
                for side in range(2):
                    piece = got[:, side * atoms:(side + 1) * atoms]
                    b = brow_ref[side * per + n]
                    for row in range(blocks):
                        acc[row] = acc[row] + jnp.where(b == row, piece, 0.0)
            return tuple(acc)

        acc = one(reach, tuple(jnp.zeros((rhs, atoms), F32) for _ in range(blocks)))

        def step(i, acc):
            for t in (reach - i, reach + i):
                ghost_copy(e, t).wait_recv()
                acc = one(t, acc)
            return acc

        acc = lax.fori_loop(1, reach + 1, step, acc)
        for row in range(blocks):
            pout_ref[e, row] = acc[row]
        part_copy(e).start()

    def diag(ref, vb, transpose):
        out = []
        for r in range(half):
            block = ref[h * half + r]
            out.append(mm(vb[r], block) if transpose else mm_t(vb[r], block))
        return jnp.stack(out)

    def returned(e):
        total = rout_ref[e, reach].astype(F32)
        for q in range(1, near):
            t = reach + (1 - 2 * (q % 2)) * ((q + 1) // 2)
            ret_copy(e, t).wait_recv()
            total = total + rin_ref[e, t].astype(F32)
        return total

    def drain(e):
        def one(t):
            ghost_copy(e, t).wait_send()
            ret_copy(e, t).wait_send()
        loop_q(one)
        full_copy(e).wait_send()
        part_copy(e).wait_send()

    def elast(v):
        e = 0
        vb = v.astype(BF16)
        full_refs[e][mine] = vb
        full_copy(e).start()
        fetch_start(e, vb)
        return vb

    def elast_end(vb, v=None):
        e = 0
        full_copy(e).wait_recv()
        transposed(e)
        dpart = diag(ediag_ref, vb, False)
        forward(e)
        part_copy(e).wait_recv()
        stored = pout_ref[e, mine] + pin_ref[e]
        finish = None
        if v is not None:
            finish = dot_start(jnp.sum(v * (dpart + 2.0 * stored), axis=0))
        total = dpart + stored + returned(e)
        drain(e)
        return total if finish is None else (total, finish())

    def factor(v, after_start=None):
        e = 1
        vb = v.astype(BF16)
        fetch_start(e, vb)
        if after_start is not None:
            after_start()
        dpart = diag(fdiag_ref, vb, False)
        forward(e)
        part_copy(e).wait_recv()
        w = dpart + (pout_ref[e, mine] + pin_ref[e])
        wb = w.astype(BF16)
        full_refs[e][mine] = wb
        full_copy(e).start()
        finish = dot_start(jnp.sum(w * wb.astype(F32), axis=0))
        dpart = diag(fdiag_ref, wb, True)
        full_copy(e).wait_recv()
        transposed(e)
        total = dpart + returned(e)
        drain(e)
        return total, finish()

    count = [0]

    def dot_start(s):
        par = count[0] % 2
        count[0] += 1
        s = jnp.concatenate([s, jnp.zeros((atoms - rhs, atoms), F32)], axis=0)
        ar_ref[par, 0] = jnp.sum(s.T, axis=0, keepdims=True)

        def copy(o, k, row, col):
            at = o * 2 + k
            return remote(ar_ref.at[par, 0], ar_ref.at[par, at], a_send.at[par, at], a_recv.at[par, at], row, col)

        each_other(lambda *to: copy(*to).start())

        def end():
            each_other(lambda *to: copy(*to).wait())
            total = jnp.sum(ar_ref[par], axis=0)
            return jnp.broadcast_to(total, (atoms, atoms)).T[:rhs]

        return end

    loads[0].wait()
    guess = guess_ref[mine]
    vb = elast(guess)
    read_lists()
    loads[1].wait()
    pick_other(0, eoff_ref)
    weights(0).start()
    loads[2].wait()
    pick_own(0, eoff_ref)
    pick_other(1, foff_ref)
    weights(1).start()
    pick_own(1, foff_ref)
    for load in loads[3:]:
        load.wait()
    weights(0).wait()
    residual = pot_ref[mine] - elast_end(vb)
    precond, rz = factor(residual, lambda: weights(1).wait())
    resid_ref[mine] = residual
    charges_ref[mine] = guess
    direction = precond
    for sweep in range(ITERS):
        image, curvature = elast_end(elast(direction), direction)
        step = rz / curvature
        charges_ref[mine] = charges_ref[mine] + step[None] * direction
        residual = resid_ref[mine] - step[None] * image
        resid_ref[mine] = residual
        if sweep + 1 < ITERS:
            precond, fresh = factor(residual)
            direction = precond + (fresh / rz)[None] * direction
            rz = fresh
    last = [
        remote(ref.at[mine], ref.at[mine], o_send.at[i], o_recv.at[i], d, sib)
        for i, ref in enumerate((charges_ref, resid_ref))
    ]
    for copy in last:
        copy.start()
    for copy in last:
        copy.wait()


def local(
    potential, charges_guess, elast_diag, elast_off, factor_diag, factor_off, block_slot, need_list
):
    rows_n = lax.axis_size("row")
    near, width = need_list.shape[2], need_list.shape[3]
    reach = (near - 1) // 2
    block_rows, slot_count = block_slot.shape
    rhs, atoms = potential.shape[1], potential.shape[2]
    slots = block_rows * slot_count
    assert slots == near * width and width == block_rows and lax.axis_size("col") == 2
    half = block_rows // 2
    per = near * half
    vmem = pl.BlockSpec(memory_space=pltpu.VMEM)
    hbm = pl.BlockSpec(memory_space=pltpu.HBM)
    group = rows_n * 2
    dma = pltpu.SemaphoreType.DMA
    shape = jax.ShapeDtypeStruct(potential.shape, F32)
    return pl.pallas_call(
        functools.partial(kernel, rows_n, near, half),
        out_shape=(shape, shape),
        in_specs=[vmem] * 2 + [hbm] * 6,
        out_specs=(vmem, vmem),
        scratch_shapes=[
            pltpu.SMEM((slots,), jnp.int32), pltpu.SMEM((slots,), jnp.int32),
            pltpu.VMEM((2, near, near + 1, atoms), jnp.int32),
            pltpu.VMEM((2 * (near + 1), atoms), jnp.int32),
            pltpu.SMEM((2 * (near + 1), atoms), jnp.int32),
            pltpu.VMEM(potential.shape, F32), pltpu.VMEM(potential.shape, F32),
            pltpu.VMEM(elast_diag.shape, BF16), pltpu.VMEM((slots, atoms, atoms), BF16),
            pltpu.VMEM(elast_diag.shape, BF16), pltpu.VMEM((slots, atoms, atoms), BF16),
            dma((6,)), dma((2, near)), dma((2, near)), dma((1,)),
            pltpu.VMEM((2, 2, per, atoms, atoms), BF16),
            pltpu.VMEM((2, per, atoms, atoms), BF16),
            pltpu.VMEM((2, near, half, rhs, atoms), BF16),
            pltpu.VMEM((block_rows, rhs, atoms), BF16),
            pltpu.VMEM((block_rows, rhs, atoms), BF16),
            pltpu.VMEM((2, near, half, rhs, atoms), BF16),
            pltpu.VMEM((2, near, half, rhs, atoms), BF16),
            pltpu.VMEM((2, block_rows, rhs, atoms), F32),
            pltpu.VMEM((2, half, rhs, atoms), F32),
            pltpu.VMEM((2, group, 1, atoms), F32),
            dma((2,)), dma((2,)),
            dma((2, near)), dma((2, near)),
            dma((2,)), dma((2,)),
            dma((2, near)), dma((2, near)),
            dma((2,)), dma((2,)),
            dma((2, group)), dma((2, group)),
            dma((2,)), dma((2,)),
        ],
        compiler_params=pltpu.CompilerParams(
            collective_id=0, has_side_effects=True, vmem_limit_bytes=63 * 1024 * 1024),
    )(
        block_slot, need_list.reshape(near, width), potential, charges_guess, elast_diag,
        elast_off.reshape(slots, atoms, atoms), factor_diag, factor_off.reshape(slots, atoms, atoms),
    )


def solution(mesh):
    return jax.shard_map(
        local,
        mesh=mesh,
        in_specs=(
            P(("grp", "row"), None, None),
            P(("grp", "row"), None, None),
            P(("grp", "row"), None, None),
            P(("grp", "row"), "col", None, None),
            P(("grp", "row"), None, None),
            P(("grp", "row"), "col", None, None),
            P(("grp", "row"), "col"),
            P(("grp", "row"), "col", None, None),
        ),
        out_specs=(P(("grp", "row"), None, None), P(("grp", "row"), None, None)),
        check_vma=False,
    )
```

```python
import functools

import jax
import jax.numpy as jnp
from jax import lax
from jax.experimental import pallas as pl
from jax.experimental.pallas import tpu as pltpu
from jax.sharding import PartitionSpec as P

ITERS = 3
F32 = jnp.float32
BF16 = jnp.bfloat16


def mm(a, b):
    return lax.dot_general(a, b, (((1,), (0,)), ((), ())), preferred_element_type=F32)


def mm_t(a, b):
    return lax.dot_general(a, b, (((1,), (1,)), ((), ())), preferred_element_type=F32)


def kernel(
    rows_n, near, half,
    slot_ref, need_ref, pot_hbm, guess_hbm, ediag_hbm, eoff_hbm, fdiag_hbm, foff_hbm,
    charges_ref, resid_ref,
    take_ref, brow_ref, msg_ref, list_ref, table_ref,
    pot_ref, guess_ref, ediag_ref, eoff_ref, fdiag_ref, foff_ref,
    in_sem, m_send, m_recv, t_sem,
    w_ref, stage_ref, ghost_ref, full_e_ref, full_f_ref, rout_ref, rin_ref, pout_ref, pin_ref, ar_ref,
    w_send, w_recv, g_send, g_recv, f_send, f_recv, r_send, r_recv, p_send, p_recv,
    a_send, a_recv, o_send, o_recv,
):
    full_refs = (full_e_ref, full_f_ref)
    d = lax.axis_index("row")
    h = lax.axis_index("col")
    sib = 1 - h
    reach = (near - 1) // 2
    group = rows_n * 2
    rhs, atoms = pot_ref.shape[1], pot_ref.shape[2]
    per = near * half
    mine = pl.ds(h * half, half)
    theirs = pl.ds(sib * half, half)

    loads = [
        pltpu.make_async_copy(src, dst, in_sem.at[i])
        for i, (src, dst) in enumerate((
            (guess_hbm, guess_ref), (eoff_hbm, eoff_ref), (foff_hbm, foff_ref),
            (pot_hbm, pot_ref), (ediag_hbm, ediag_ref), (fdiag_hbm, fdiag_ref)))
    ]
    for load in loads:
        load.start()

    barrier = pltpu.get_barrier_semaphore()

    def wrap(x):
        return jnp.where(x < 0, x + rows_n, jnp.where(x >= rows_n, x - rows_n, x))

    cols = (h, sib)

    def each_other(body):
        body(0, 1, d, sib)
        if rows_n <= 8:
            for o in range(1, rows_n):
                for k in range(2):
                    body(o, k, wrap(d + o), cols[k])
        else:
            def step(o, c):
                for k in range(2):
                    body(o, k, wrap(d + o), cols[k])
                return c
            lax.fori_loop(1, rows_n, step, 0)

    def greet(o, k, row, col):
        pl.semaphore_signal(
            barrier, inc=1, device_id={"row": row, "col": col},
            device_id_type=pl.DeviceIdType.MESH)

    each_other(greet)

    def pick_other(m, off_ref):
        def body(n, c):
            stage_ref[m, n] = off_ref[take_ref[per + n]]
            return c
        lax.fori_loop(0, per, body, 0)

    def pick_own(m, off_ref):
        def body(n, c):
            w_ref[m, 0, n] = off_ref[take_ref[n]]
            return c
        lax.fori_loop(0, per, body, 0)

    def remote(src, dst, ssem, rsem, row, col):
        return pltpu.make_async_remote_copy(
            src_ref=src, dst_ref=dst, send_sem=ssem, recv_sem=rsem,
            device_id={"row": row, "col": col}, device_id_type=pl.DeviceIdType.MESH)

    def weights(m):
        return remote(stage_ref.at[m], w_ref.at[m, 1], w_send.at[m], w_recv.at[m], d, sib)

    block_rows, slot_count = slot_ref.shape
    width = need_ref.shape[1]
    lane = lax.broadcasted_iota(jnp.int32, (block_rows, atoms), 1)
    line = lax.broadcasted_iota(jnp.int32, (block_rows, atoms), 0)
    pad = 1 << (slot_count - 1).bit_length()
    slot_at = jnp.zeros((block_rows, atoms), jnp.int32)
    for k in range(slot_count):
        slot_at = slot_at + jnp.where(slot_ref[:, k:k + 1] == lane, line * pad + k, 0)
    slot_at = jnp.sum(slot_at, axis=0, keepdims=True)
    lane = lax.broadcasted_iota(jnp.int32, (near, atoms), 1)
    place = jnp.zeros((near, atoms), jnp.int32)
    for j in range(width):
        place = place + jnp.where(need_ref[:, j:j + 1] == lane, j, 0)
    msg_ref[0, reach] = jnp.concatenate([place, slot_at], axis=0)

    def msg_copy(k, t):
        row = wrap(d + reach - t)
        return remote(msg_ref.at[0, reach], msg_ref.at[k, t], m_send.at[k, t], m_recv.at[k, t],
                      row, cols[k])

    messages = [(k, t) for k in range(2) for t in range(near) if (k, t) != (0, reach)]

    def read_lists():
        for k, t in messages:
            msg_copy(k, t).wait()
        list_ref[...] = jnp.concatenate(
            [line for k in range(2)
             for line in [msg_ref[k, t, t:t + 1] for t in range(near)] + [msg_ref[k, reach, near:near + 1]]],
            axis=0)
        copy = pltpu.make_async_copy(list_ref, table_ref, t_sem.at[0])
        copy.start()
        copy.wait()

        def slot_of(k, t, side, r):
            at = jnp.clip(table_ref[k * (near + 1) + t, side * half + r], 0, width - 1)
            code = table_ref[k * (near + 1) + near, t * width + at]
            row = jnp.clip(lax.shift_right_arithmetic(code, shift), 0, block_rows - 1)
            return jnp.clip(code - row * (pad - slot_count), 0, 2 * per - 1), row

        shift = pad.bit_length() - 1
        for t in range(near):
            for r in range(half):
                n = t * half + r
                take_ref[n], brow_ref[n] = slot_of(0, t, h, r)
                take_ref[per + n] = slot_of(0, t, sib, r)[0]
                brow_ref[per + n] = slot_of(1, t, h, r)[1]

    pl.semaphore_wait(barrier, group - 1)
    for k, t in messages:
        msg_copy(k, t).start()

    def ghost_copy(e, t):
        row = wrap(d + reach - t)
        return remote(ghost_ref.at[e, reach], ghost_ref.at[e, t], g_send.at[e, t], g_recv.at[e, t], row, h)

    def full_copy(e):
        return remote(full_refs[e].at[mine], full_refs[e].at[mine], f_send.at[e], f_recv.at[e], d, sib)

    def ret_copy(e, t):
        row = wrap(d + t - reach)
        return remote(rout_ref.at[e, t], rin_ref.at[e, t], r_send.at[e, t], r_recv.at[e, t], row, h)

    def part_copy(e):
        return remote(pout_ref.at[e, theirs], pin_ref.at[e], p_send.at[e], p_recv.at[e], d, sib)

    def loop_q(body):
        def step(i, c):
            body(i - 1)
            body(near - i)
            return c
        lax.fori_loop(1, reach + 1, step, 0)

    def fetch_start(e, vb):
        ghost_ref[e, reach] = vb
        for i in range(reach):
            ghost_copy(e, i).start()
            ghost_copy(e, near - 1 - i).start()

    def transposed(e):
        def one(t):
            for r in range(half):
                n = t * half + r
                first = mm(full_refs[e][brow_ref[n]], w_ref[e, 0, n]).astype(BF16).astype(F32)
                second = mm(full_refs[e][brow_ref[per + n]], w_ref[e, 1, n]).astype(BF16).astype(F32)
                rout_ref[e, t, r] = (first + second).astype(BF16)

        def far(t):
            one(t)
            ret_copy(e, t).start()
        loop_q(far)
        one(reach)

    def forward(e):
        blocks = 2 * half

        def one(t, acc):
            acc = list(acc)
            for r in range(half):
                n = t * half + r
                both = jnp.concatenate([w_ref[e, 0, n], w_ref[e, 1, n]], axis=0)
                got = mm_t(ghost_ref[e, t, r], both)
                for side in range(2):
                    piece = got[:, side * atoms:(side + 1) * atoms]
                    b = brow_ref[side * per + n]
                    for row in range(blocks):
                        acc[row] = acc[row] + jnp.where(b == row, piece, 0.0)
            return tuple(acc)

        acc = one(reach, tuple(jnp.zeros((rhs, atoms), F32) for _ in range(blocks)))

        def step(i, acc):
            for t in (i - 1, near - i):
                ghost_copy(e, t).wait_recv()
                acc = one(t, acc)
            return acc

        acc = lax.fori_loop(1, reach + 1, step, acc)
        for row in range(blocks):
            pout_ref[e, row] = acc[row]
        part_copy(e).start()

    def diag(ref, vb, transpose):
        out = []
        for r in range(half):
            block = ref[h * half + r]
            out.append(mm(vb[r], block) if transpose else mm_t(vb[r], block))
        return jnp.stack(out)

    def returned(e):
        total = rout_ref[e, reach].astype(F32)
        for q in range(1, near):
            t = reach + (1 - 2 * (q % 2)) * ((q + 1) // 2)
            ret_copy(e, t).wait_recv()
            total = total + rin_ref[e, t].astype(F32)
        return total

    def drain(e):
        def one(t):
            ghost_copy(e, t).wait_send()
            ret_copy(e, t).wait_send()
        loop_q(one)
        full_copy(e).wait_send()
        part_copy(e).wait_send()

    def elast(v):
        e = 0
        vb = v.astype(BF16)
        full_refs[e][mine] = vb
        full_copy(e).start()
        fetch_start(e, vb)
        return vb

    def elast_end(vb, v=None):
        e = 0
        full_copy(e).wait_recv()
        transposed(e)
        dpart = diag(ediag_ref, vb, False)
        forward(e)
        part_copy(e).wait_recv()
        stored = pout_ref[e, mine] + pin_ref[e]
        finish = None
        if v is not None:
            finish = dot_start(jnp.sum(v * (dpart + 2.0 * stored), axis=0))
        total = dpart + stored + returned(e)
        drain(e)
        return total if finish is None else (total, finish())

    def factor(v, after_start=None):
        e = 1
        vb = v.astype(BF16)
        fetch_start(e, vb)
        if after_start is not None:
            after_start()
        dpart = diag(fdiag_ref, vb, False)
        forward(e)
        part_copy(e).wait_recv()
        w = dpart + (pout_ref[e, mine] + pin_ref[e])
        wb = w.astype(BF16)
        full_refs[e][mine] = wb
        full_copy(e).start()
        finish = dot_start(jnp.sum(w * wb.astype(F32), axis=0))
        dpart = diag(fdiag_ref, wb, True)
        full_copy(e).wait_recv()
        transposed(e)
        total = dpart + returned(e)
        drain(e)
        return total, finish()

    count = [0]

    def dot_start(s):
        par = count[0] % 2
        count[0] += 1
        s = jnp.concatenate([s, jnp.zeros((atoms - rhs, atoms), F32)], axis=0)
        ar_ref[par, 0] = jnp.sum(s.T, axis=0, keepdims=True)

        def copy(o, k, row, col):
            at = o * 2 + k
            return remote(ar_ref.at[par, 0], ar_ref.at[par, at], a_send.at[par, at], a_recv.at[par, at], row, col)

        each_other(lambda *to: copy(*to).start())

        def end():
            each_other(lambda *to: copy(*to).wait())
            total = jnp.sum(ar_ref[par], axis=0)
            return jnp.broadcast_to(total, (atoms, atoms)).T[:rhs]

        return end

    loads[0].wait()
    guess = guess_ref[mine]
    vb = elast(guess)
    read_lists()
    loads[1].wait()
    pick_other(0, eoff_ref)
    weights(0).start()
    loads[2].wait()
    pick_own(0, eoff_ref)
    pick_other(1, foff_ref)
    weights(1).start()
    pick_own(1, foff_ref)
    for load in loads[3:]:
        load.wait()
    weights(0).wait()
    residual = pot_ref[mine] - elast_end(vb)
    precond, rz = factor(residual, lambda: weights(1).wait())
    resid_ref[mine] = residual
    charges_ref[mine] = guess
    direction = precond
    for sweep in range(ITERS):
        image, curvature = elast_end(elast(direction), direction)
        step = rz / curvature
        charges_ref[mine] = charges_ref[mine] + step[None] * direction
        residual = resid_ref[mine] - step[None] * image
        resid_ref[mine] = residual
        if sweep + 1 < ITERS:
            precond, fresh = factor(residual)
            direction = precond + (fresh / rz)[None] * direction
            rz = fresh
    last = [
        remote(ref.at[mine], ref.at[mine], o_send.at[i], o_recv.at[i], d, sib)
        for i, ref in enumerate((charges_ref, resid_ref))
    ]
    for copy in last:
        copy.start()
    for copy in last:
        copy.wait()


def local(
    potential, charges_guess, elast_diag, elast_off, factor_diag, factor_off, block_slot, need_list
):
    rows_n = lax.axis_size("row")
    near, width = need_list.shape[2], need_list.shape[3]
    reach = (near - 1) // 2
    block_rows, slot_count = block_slot.shape
    rhs, atoms = potential.shape[1], potential.shape[2]
    slots = block_rows * slot_count
    assert slots == near * width and width == block_rows and lax.axis_size("col") == 2
    half = block_rows // 2
    per = near * half
    vmem = pl.BlockSpec(memory_space=pltpu.VMEM)
    hbm = pl.BlockSpec(memory_space=pltpu.HBM)
    group = rows_n * 2
    dma = pltpu.SemaphoreType.DMA
    shape = jax.ShapeDtypeStruct(potential.shape, F32)
    return pl.pallas_call(
        functools.partial(kernel, rows_n, near, half),
        out_shape=(shape, shape),
        in_specs=[vmem] * 2 + [hbm] * 6,
        out_specs=(vmem, vmem),
        scratch_shapes=[
            pltpu.SMEM((slots,), jnp.int32), pltpu.SMEM((slots,), jnp.int32),
            pltpu.VMEM((2, near, near + 1, atoms), jnp.int32),
            pltpu.VMEM((2 * (near + 1), atoms), jnp.int32),
            pltpu.SMEM((2 * (near + 1), atoms), jnp.int32),
            pltpu.VMEM(potential.shape, F32), pltpu.VMEM(potential.shape, F32),
            pltpu.VMEM(elast_diag.shape, BF16), pltpu.VMEM((slots, atoms, atoms), BF16),
            pltpu.VMEM(elast_diag.shape, BF16), pltpu.VMEM((slots, atoms, atoms), BF16),
            dma((6,)), dma((2, near)), dma((2, near)), dma((1,)),
            pltpu.VMEM((2, 2, per, atoms, atoms), BF16),
            pltpu.VMEM((2, per, atoms, atoms), BF16),
            pltpu.VMEM((2, near, half, rhs, atoms), BF16),
            pltpu.VMEM((block_rows, rhs, atoms), BF16),
            pltpu.VMEM((block_rows, rhs, atoms), BF16),
            pltpu.VMEM((2, near, half, rhs, atoms), BF16),
            pltpu.VMEM((2, near, half, rhs, atoms), BF16),
            pltpu.VMEM((2, block_rows, rhs, atoms), F32),
            pltpu.VMEM((2, half, rhs, atoms), F32),
            pltpu.VMEM((2, group, 1, atoms), F32),
            dma((2,)), dma((2,)),
            dma((2, near)), dma((2, near)),
            dma((2,)), dma((2,)),
            dma((2, near)), dma((2, near)),
            dma((2,)), dma((2,)),
            dma((2, group)), dma((2, group)),
            dma((2,)), dma((2,)),
        ],
        compiler_params=pltpu.CompilerParams(
            collective_id=0, has_side_effects=True, vmem_limit_bytes=63 * 1024 * 1024),
    )(
        block_slot, need_list.reshape(near, width), potential, charges_guess, elast_diag,
        elast_off.reshape(slots, atoms, atoms), factor_diag, factor_off.reshape(slots, atoms, atoms),
    )


def solution(mesh):
    return jax.shard_map(
        local,
        mesh=mesh,
        in_specs=(
            P(("grp", "row"), None, None),
            P(("grp", "row"), None, None),
            P(("grp", "row"), None, None),
            P(("grp", "row"), "col", None, None),
            P(("grp", "row"), None, None),
            P(("grp", "row"), "col", None, None),
            P(("grp", "row"), "col"),
            P(("grp", "row"), "col", None, None),
        ),
        out_specs=(P(("grp", "row"), None, None), P(("grp", "row"), None, None)),
        check_vma=False,
    )
```
